32 devices in a mesh: row: 8 (over z, y), col: 4 (over x, core).
Axes of the slice: x: 2, y: 2, z: 4, core: 2. Of those that a mesh axis runs over, the one named last changes fastest.
Arguments:
- anc_inverse: float32 [16384, 16384], P('row', 'col')
- panel: float32 [1920, 2560], P('row', 'col'), may hold values from -0.015625 to 0.015625
- local_rows: int32 [1920], P('row'), may hold values from -1 to 2047, as said below
- inv_diag: float32 [2560, 2560], P('row', 'col')
Outputs:
- sigma_off: float32 [1920, 2560], P('row', 'col')
- sigma_diag: float32 [2560, 2560], P('row', 'col')
The draws below stay inside these ranges and needn't reach their ends.
Inputs may be any that keep to these rules, and one draw needn't show every extreme that they name: `local_rows`: each aligned block of 240 slots lists its live ancestor rows first, distinct and ascending, then -1 in the rest; every block has at least one live slot, some block is full and some block is at most half full.
All inputs are finite; a program needn't handle non-finite values.
Results may differ from the reference program's by a relative error of at most 0.000075.
Values sent between devices are 32-bit elements; how exact they have to be, the bound alone decides.
No kernel may reach another device: no remote copies, remote signals or barrier semaphores. Data moves between devices by JAX's collectives and lax.ppermute only.
A program may use at most 128 MiB of HBM per device.

```python
import math
import jax
import jax.numpy as jnp
from jax import lax

NA = 16384
NJ = 2560
CAP = 240
ANC_ROWS = 2048
SLOTS = 1920


def draw_anc_inverse(key, part):
    first_key, second_key = jax.random.split(key)
    noise = jax.random.normal(first_key, (NA, NA), jnp.float32)
    lift = 1.0 + jax.random.uniform(second_key, (NA,), jnp.float32)
    scale_off = 0.7071 * SLOTS / math.sqrt(NA)
    offdiag = (noise + noise.T) * scale_off
    diag_index = jnp.arange(NA)
    return offdiag.at[diag_index, diag_index].add(SLOTS * lift)


def draw_inv_diag(key, part):
    first_key, second_key = jax.random.split(key)
    noise = jax.random.normal(first_key, (NJ, NJ), jnp.float32)
    lift = 1.0 + jax.random.uniform(second_key, (NJ,), jnp.float32)
    diag_index = jnp.arange(NJ)
    return ((noise + noise.T) * 0.35).at[diag_index, diag_index].add(lift)


def draw_local_rows(key, part):
    blocks = SLOTS // CAP
    count_key, full_key, perm_key = jax.random.split(jax.random.fold_in(key, 7), 3)
    counts = jax.random.randint(count_key, (blocks,), CAP // 2, CAP + 1)
    full_block = jax.random.randint(full_key, (), 0, blocks)
    half_block = (full_block + 1) % blocks
    block_ids = jnp.arange(blocks)
    counts = jnp.where(block_ids == full_block, CAP, counts)
    counts = jnp.where(block_ids == half_block, CAP // 2, counts)
    perm_keys = jax.random.split(perm_key, blocks)
    perms = jax.vmap(lambda one_key: jax.random.permutation(one_key, ANC_ROWS))(perm_keys)
    first_vals = perms[:, :1]
    swapped = jnp.where(perms == ANC_ROWS - 1, first_vals, perms)
    swapped = swapped.at[:, 0].set(ANC_ROWS - 1)
    perms = jnp.where((block_ids == full_block)[:, None], swapped, perms)[:, :CAP]
    position = jnp.arange(CAP)
    live = position[None, :] < counts[:, None]
    chosen = jnp.sort(jnp.where(live, perms, ANC_ROWS + 1), axis=1)
    result = jnp.where(chosen > ANC_ROWS, -1, chosen)
    return result.reshape(-1).astype(jnp.int32)


def shard_levels(rng, extent, cuts, smallest, largest):
    loudness = 1.0
    for dim, parts in cuts:
        draws = jax.random.uniform(jax.random.fold_in(jax.random.fold_in(rng, 6), dim), (parts,), jnp.float32, smallest / len(cuts), largest / len(cuts))
        loudness = loudness * jnp.repeat(jnp.exp(draws), extent[dim] // parts).reshape((-1,) + (1,) * (len(extent) - 1 - dim))
    return loudness


def bell_draw(rng, dims, scale, reach, pieces=(), kind=jnp.bfloat16):
    factor_of = shard_levels(rng, dims, pieces, -0.22, 0.18) if pieces else 1.0
    drawn = jax.random.normal(rng, dims, jnp.float32) * scale * factor_of
    return jnp.minimum(jnp.maximum(drawn, -reach), reach).astype(kind)


def setup_inputs(seed: int = 0) -> dict:
    splits = jax.random.split(jax.random.key(seed), 5)
    anc_inverse = draw_anc_inverse(jax.random.fold_in(splits[4], 71), 0)
    panel = bell_draw(splits[1], (SLOTS, NJ), (2.0 * SLOTS ** -1), 0.015625, ((0, 8), (1, 4)), jnp.float32)
    local_rows = draw_local_rows(jax.random.fold_in(splits[4], 71), 0)
    inv_diag = draw_inv_diag(jax.random.fold_in(splits[4], 71), 0)
    return dict(anc_inverse=anc_inverse, panel=panel, local_rows=local_rows, inv_diag=inv_diag)


def reference(anc_inverse, panel, local_rows, inv_diag):
    slot_count = local_rows.shape[0]
    block_of = jnp.arange(slot_count, dtype=jnp.int32) // CAP
    live = (local_rows >= 0).astype(jnp.float32)
    anc = (block_of * ANC_ROWS + jnp.maximum(local_rows, 0)).astype(jnp.int32)
    picked = jnp.take(anc_inverse, anc, axis=0)
    compact = jnp.take(picked, anc, axis=1) * live[:, None] * live[None, :]
    sigma_off = -jnp.dot(compact, panel, precision=lax.Precision.HIGHEST)
    sigma_diag = inv_diag - jnp.dot(panel.T, sigma_off, precision=lax.Precision.HIGHEST)
    return sigma_off, sigma_diag
```

```python
import functools

import jax
import jax.numpy as jnp
from jax import lax
from jax.experimental import pallas as pl
from jax.experimental.pallas import tpu as pltpu
from jax.sharding import PartitionSpec as P

MEMBERS = 2
BF16 = jnp.bfloat16
F32 = jnp.float32


def split(x):
    high = x.astype(BF16)
    return high, (x - high.astype(F32)).astype(BF16)


def dot(a, b):
    return jnp.dot(a, b, preferred_element_type=F32)


def dot3(a, b):
    return dot(a[0], b[0]) + (dot(a[0], b[1]) + dot(a[1], b[0]))


def whole(*shape):
    return pl.BlockSpec(shape, lambda *_: (0,) * len(shape))


def params():
    return pltpu.CompilerParams(vmem_limit_bytes=48 * 2**20)


def cost(flops, moved):
    return pl.CostEstimate(flops=flops, bytes_accessed=moved, transcendentals=0)


def pick_kernel(rows_ref, member_ref, anc, own_ref, lists_ref, keep_ref, send_ref, picked, sem):
    count, width = picked.shape[0], picked.shape[1] // MEMBERS

    def fetch(i, carry):
        row = jnp.maximum(rows_ref[i], 0)
        pltpu.make_async_copy(anc.at[pl.ds(row, 1), :], picked.at[pl.ds(i, 1), :], sem).start()
        return carry

    lax.fori_loop(0, count, fetch, 0, unroll=8)
    pltpu.make_async_copy(anc.at[pl.ds(0, count), :], picked, sem).wait()
    live = own_ref[...] >= 0
    ancestor = lax.broadcasted_iota(jnp.int32, (width, count), 0)
    for k, out in enumerate((keep_ref, send_ref)):
        member = jnp.bitwise_xor(member_ref[0], k)
        region = picked[:, pl.ds(pl.multiple_of(member * width, 128), width)]
        high, low = split(region)
        chosen = (ancestor == lists_ref[k : k + 1, :]).astype(BF16)
        out[...] = jnp.where(live, dot(high, chosen) + dot(low, chosen), 0.0)


def pick(anc, rows, member, lists):
    count, width = rows.shape[0], anc.shape[1]
    square = jax.ShapeDtypeStruct((count, count), F32)
    return pl.pallas_call(
        pick_kernel,
        grid_spec=pltpu.PrefetchScalarGridSpec(
            num_scalar_prefetch=2,
            grid=(1,),
            in_specs=[pl.BlockSpec(memory_space=pl.ANY), whole(count, 1), whole(MEMBERS, count)],
            out_specs=[whole(count, count)] * 2,
            scratch_shapes=[pltpu.VMEM((count, width), F32), pltpu.SemaphoreType.DMA],
        ),
        out_shape=(square, square),
        compiler_params=params(),
        cost_estimate=cost(4 * count * count * width, 4 * count * width),
        name="pick_compact",
    )(rows, member, anc, rows[:, None], lists)


def off_kernel(order_ref, pieces_ref, *refs):
    blocks, (own_ref, other_ref) = refs[:-2], refs[-2:]
    count = own_ref.shape[0]
    total = None
    for step, block in enumerate(blocks):
        term = dot3(split(pieces_ref[order_ref[step]]), split(block[...]))
        total = term if total is None else total + term
    own_ref[...] = -total[:count]
    other_ref[...] = -total[count:]


def off_parts(order, pieces, blocks):
    count, width = blocks[0].shape
    out = jax.ShapeDtypeStruct((count, width), F32)
    return pl.pallas_call(
        off_kernel,
        grid_spec=pltpu.PrefetchScalarGridSpec(
            num_scalar_prefetch=1,
            grid=(1,),
            in_specs=[whole(*pieces.shape)] + [whole(count, width)] * len(blocks),
            out_specs=[whole(count, width)] * 2,
        ),
        out_shape=(out, out),
        compiler_params=params(),
        cost_estimate=cost(12 * count * count * width * len(blocks), 4 * pieces.size),
        name="off_parts",
    )(order, pieces, *blocks)


def diag_kernel(member_ref, *refs):
    count = (len(refs) - 3) // 2
    strips, blocks, (own_ref, other_ref, total) = refs[:count], refs[count : 2 * count], refs[2 * count :]
    half = own_ref.shape[0]
    for step in range(count):
        strip = split(strips[step][...].T)
        term = dot3(strip, split(blocks[step][...]))
        total[...] = term if step == 0 else total[...] + term
    mine = pl.multiple_of(member_ref[0] * half, 8)
    own_ref[...] = total[pl.ds(mine, half), :]
    other_ref[...] = total[pl.ds(pl.multiple_of(half - mine, 8), half), :]


def diag_parts(member, strips, blocks):
    (count, strip_width), width = strips[0].shape, blocks[0].shape[1]
    half = strip_width // MEMBERS
    out = jax.ShapeDtypeStruct((half, width), F32)
    return pl.pallas_call(
        diag_kernel,
        grid_spec=pltpu.PrefetchScalarGridSpec(
            num_scalar_prefetch=1,
            grid=(1,),
            in_specs=[whole(count, strip_width)] * len(strips) + [whole(count, width)] * len(blocks),
            out_specs=[whole(half, width)] * 2,
            scratch_shapes=[pltpu.VMEM((strip_width, width), F32)],
        ),
        out_shape=(out, out),
        compiler_params=params(),
        cost_estimate=cost(6 * count * strip_width * width * len(blocks), 4 * count * strip_width * len(blocks)),
        name="diag_parts",
    )(member, *strips, *blocks)


def shards(planes, cols, anc_inverse, panel, local_rows, inv_diag):
    axes = ("row", "col")
    row, col = lax.axis_index("row"), lax.axis_index("col")
    plane, member = row // MEMBERS, row % MEMBERS
    grid = [(z, y, c) for z in range(planes) for y in range(MEMBERS) for c in range(cols)]

    def place(z, y, c):
        return (z * MEMBERS + y) * cols + c

    def move(x, target, some=lambda z, y, c: True):
        return lax.ppermute(x, axes, [(place(*d), place(*target(*d))) for d in grid if some(*d)])

    def to_partner(x):
        return move(x, lambda z, y, c: (z, 1 - y, c))

    def round_planes(x):
        out = [x]
        for _ in range(planes - 1):
            out.append(move(out[-1], lambda z, y, c: ((z + 1) % planes, y, c)))
        return out

    def broadcast_strip(x):
        holders, apart = [0], cols // 2
        while apart:
            come = move(x, lambda z, y, c: (z, y, c ^ apart), lambda z, y, c: (c ^ z) in holders)
            has = functools.reduce(jnp.logical_or, [(col ^ plane) == h for h in holders])
            x = jnp.where(has, x, come)
            holders, apart = holders + [h ^ apart for h in holders], apart // 2
        return x

    width = panel.shape[1]
    cut = max(1, round(0.6 * width / 128)) * 128
    cuts = [(0, cut), (cut, width)] if cut < width else [(0, width)]

    lists = jnp.stack([local_rows, to_partner(local_rows)])
    lists = move(lists, lambda z, y, c: (c, y, z))
    keep, send = pick(anc_inverse, local_rows, member[None], lists)
    pieces = jnp.concatenate([keep, to_partner(send)])[None]
    apart, order = cols // 2, [0]
    while apart:
        pieces = jnp.concatenate([pieces, move(pieces, lambda z, y, c: (z, y, c ^ apart))])
        order, apart = order + [k ^ apart for k in order], apart // 2
    where = jnp.zeros((cols,), jnp.int32).at[jnp.array(order)].set(jnp.arange(cols, dtype=jnp.int32))
    wanted = where[col ^ ((plane - jnp.arange(planes, dtype=jnp.int32)) % planes)]

    panels = [round_planes(panel[:, a:b]) for a, b in cuts]
    strips = [broadcast_strip(panel)]
    for step in range(1, planes):
        strips.append(broadcast_strip(jnp.concatenate([part[step] for part in panels], axis=1)))
    off, diag = [], []
    for part in panels:
        own, other = off_parts(wanted, pieces, part)
        off.append(own + to_partner(other))
    for part in off:
        own, other = diag_parts(member[None], strips, round_planes(part))
        diag.append(own + to_partner(other))
    return jnp.concatenate(off, axis=1), inv_diag - jnp.concatenate(diag, axis=1)


def solution(mesh):
    rows, cols = mesh.shape["row"], mesh.shape["col"]
    placed = (P("row", "col"), P("row", "col"), P("row"), P("row", "col"))
    return jax.shard_map(
        functools.partial(shards, rows // MEMBERS, cols),
        mesh=mesh,
        in_specs=placed,
        out_specs=(P("row", "col"), P("row", "col")),
        check_vma=False,
    )
```

```python
import functools

import jax
import jax.numpy as jnp
from jax import lax
from jax.experimental import pallas as pl
from jax.experimental.pallas import tpu as pltpu
from jax.sharding import PartitionSpec as P

MEMBERS = 2
CUT = 0.6
GATED = 3
BF16 = jnp.bfloat16
F32 = jnp.float32


def split(x):
    high = x.astype(BF16)
    return high, (x - high.astype(F32)).astype(BF16)


def dot(a, b):
    return jnp.dot(a, b, preferred_element_type=F32)


def dot3(a, b):
    return dot(a[0], b[0]) + (dot(a[0], b[1]) + dot(a[1], b[0]))


def whole(*shape):
    return pl.BlockSpec(shape, lambda *_: (0,) * len(shape))


def params():
    return pltpu.CompilerParams(vmem_limit_bytes=48 * 2**20)


def cost(flops, moved):
    return pl.CostEstimate(flops=flops, bytes_accessed=moved, transcendentals=0)


def pick_kernel(rows_ref, member_ref, anc, own_ref, lists_ref, keep_ref, send_ref, picked, sem):
    count, width = picked.shape[0], picked.shape[1] // MEMBERS

    def fetch(i, carry):
        row = jnp.where(rows_ref[i] < 0, i, rows_ref[i])
        pltpu.make_async_copy(anc.at[pl.ds(row, 1), :], picked.at[pl.ds(i, 1), :], sem).start()
        return carry

    lax.fori_loop(0, count, fetch, 0, unroll=8)
    live = own_ref[...] >= 0
    ancestor = lax.broadcasted_iota(jnp.int32, (width, count), 0)
    chosen = [(ancestor == lists_ref[k : k + 1, :]).astype(BF16) for k in range(MEMBERS)]
    pltpu.make_async_copy(anc.at[pl.ds(0, count), :], picked, sem).wait()
    for k, out in enumerate((keep_ref, send_ref)):
        member = jnp.bitwise_xor(member_ref[0], k)
        high, low = split(picked[:, pl.ds(pl.multiple_of(member * width, 128), width)])
        out[...] = jnp.where(live, dot(high, chosen[k]) + dot(low, chosen[k]), 0.0)


def pick(anc, rows, member, lists):
    count, width = rows.shape[0], anc.shape[1]
    square = jax.ShapeDtypeStruct((count, count), F32)
    return pl.pallas_call(
        pick_kernel,
        grid_spec=pltpu.PrefetchScalarGridSpec(
            num_scalar_prefetch=2,
            grid=(1,),
            in_specs=[pl.BlockSpec(memory_space=pl.ANY), whole(count, 1), whole(MEMBERS, count)],
            out_specs=[whole(count, count)] * 2,
            scratch_shapes=[pltpu.VMEM((count, width), F32), pltpu.SemaphoreType.DMA],
        ),
        out_shape=(square, square),
        compiler_params=params(),
        cost_estimate=cost(4 * count * count * width, 16 * count * width),
        name="pick_compact",
    )(rows, member, anc, rows[:, None], lists)


def off_kernel(count, order_ref, *refs):
    own, other, blocks, (own_ref, other_ref) = refs[:count], refs[count : 2 * count], refs[2 * count : -2], refs[-2:]
    rows = own_ref.shape[0]
    total = None
    for step, block in enumerate(blocks):
        piece = jnp.concatenate([own[0][...], other[0][...]])
        for k in range(1, count):
            piece = jnp.where(order_ref[step] == k, jnp.concatenate([own[k][...], other[k][...]]), piece)
        term = dot3(split(piece), split(block[...]))
        total = term if total is None else total + term
    own_ref[...] = -total[:rows]
    other_ref[...] = -total[rows:]


def off_parts(order, own, other, blocks):
    count, width = blocks[0].shape
    out = jax.ShapeDtypeStruct((count, width), F32)
    return pl.pallas_call(
        functools.partial(off_kernel, len(own)),
        grid_spec=pltpu.PrefetchScalarGridSpec(
            num_scalar_prefetch=1,
            grid=(1,),
            in_specs=[whole(*x.shape) for x in (*own, *other, *blocks)],
            out_specs=[whole(count, width)] * 2,
        ),
        out_shape=(out, out),
        compiler_params=params(),
        cost_estimate=cost(12 * count * count * width * len(blocks), 8 * count * count * len(blocks)),
        name="off_parts",
    )(order, *own, *other, *blocks)


def turn_kernel(flag_ref, held, come, high_ref, low_ref):
    strip = jnp.where(flag_ref[0] > 0, held[...], come[...]).T
    high_ref[...], low_ref[...] = split(strip)


def turn(flag, held, come):
    count, width = held.shape
    out = jax.ShapeDtypeStruct((width, count), BF16)
    return pl.pallas_call(
        turn_kernel,
        grid_spec=pltpu.PrefetchScalarGridSpec(
            num_scalar_prefetch=1,
            grid=(1,),
            in_specs=[whole(count, width)] * 2,
            out_specs=[whole(width, count)] * 2,
        ),
        out_shape=(out, out),
        compiler_params=params(),
        cost_estimate=cost(0, 12 * count * width),
        name="turn_strip",
    )(flag, held, come)


def diag_kernel(start, member_ref, base_ref, *refs):
    count = (len(refs) - 3) // 3
    highs, lows, blocks = refs[:count], refs[count : 2 * count], refs[2 * count : -3]
    own_ref, other_ref, total = refs[-3:]
    half, width = own_ref.shape
    for step in range(count):
        term = dot3((highs[step][...], lows[step][...]), split(blocks[step][...]))
        total[...] = term if step == 0 else total[...] + term
    mine = pl.multiple_of(member_ref[0] * half, 8)
    own_ref[...] = base_ref[:, start : start + width] - total[pl.ds(mine, half), :]
    other_ref[...] = total[pl.ds(pl.multiple_of(half - mine, 8), half), :]


def diag_parts(member, base, start, strips, blocks):
    (strip_width, count), width = strips[0][0].shape, blocks[0].shape[1]
    half = strip_width // MEMBERS
    flat = [base, *(high for high, _ in strips), *(low for _, low in strips), *blocks]
    out = jax.ShapeDtypeStruct((half, width), F32)
    return pl.pallas_call(
        functools.partial(diag_kernel, start),
        grid_spec=pltpu.PrefetchScalarGridSpec(
            num_scalar_prefetch=1,
            grid=(1,),
            in_specs=[whole(*x.shape) for x in flat],
            out_specs=[whole(half, width)] * 2,
            scratch_shapes=[pltpu.VMEM((strip_width, width), F32)],
        ),
        out_shape=(out, out),
        compiler_params=params(),
        cost_estimate=cost(6 * count * strip_width * width * len(blocks), 4 * count * strip_width * len(blocks)),
        name="diag_parts",
    )(member, *flat)


def shards(planes, cols, anc_inverse, panel, local_rows, inv_diag):
    axes = ("row", "col")
    row, col = lax.axis_index("row"), lax.axis_index("col")
    plane, member = row // MEMBERS, row % MEMBERS
    grid = [(z, y, c) for z in range(planes) for y in range(MEMBERS) for c in range(cols)]

    def place(z, y, c):
        return (z * MEMBERS + y) * cols + c

    def move(x, target, some=lambda z, y, c: True):
        return lax.ppermute(x, axes, [(place(*d), place(*target(*d))) for d in grid if some(*d)])

    def to_partner(x):
        return move(x, lambda z, y, c: (z, 1 - y, c))

    def onward(x):
        return move(x, lambda z, y, c: ((z + 1) % planes, y, c))

    def sync(*values):
        return list(lax.optimization_barrier(values))

    class Strip:
        def __init__(self, block):
            self.block, self.holders, self.apart = block, [0], cols // 2

        def hop(self):
            apart, holders = self.apart, self.holders
            self.come = move(self.block, lambda z, y, c: (z, y, c ^ apart), lambda z, y, c: (c ^ z) in holders)

        def keep(self):
            has = functools.reduce(jnp.logical_or, [(col ^ plane) == h for h in self.holders])
            if self.apart == 1:
                return turn(has.astype(jnp.int32)[None], self.block, self.come)
            self.block = jnp.where(has, self.block, self.come)
            self.holders = self.holders + [h ^ self.apart for h in self.holders]
            self.apart //= 2

        def rest(self):
            while True:
                self.hop()
                if done := self.keep():
                    return done

    width = panel.shape[1]
    cut = max(1, round(CUT * width / 128)) * 128
    cuts = [(0, cut), (cut, width)] if cut < width else [(0, width)]
    panels = [[panel[:, a:b]] for a, b in cuts]
    panels[0].append(onward(panels[0][0]))
    lists = jnp.stack([move(local_rows, lambda z, y, c: (c, y, z)), move(local_rows, lambda z, y, c: (c, 1 - y, z))])
    keep, send = pick(anc_inverse, local_rows, member[None], lists)
    send, panels[0][1] = sync(send, panels[0][1])
    apart, order = cols // 2, [0, cols // 2]
    own = [keep, move(keep, lambda z, y, c: (z, y, c ^ apart))]
    other = [to_partner(send), move(send, lambda z, y, c: (z, 1 - y, c ^ apart))]
    while apart > 1:
        apart //= 2
        for held in (own, other):
            held += [move(piece, lambda z, y, c: (z, y, c ^ apart)) for piece in held]
        order = order + [k ^ apart for k in order]
    wanted = col ^ ((plane - jnp.arange(planes, dtype=jnp.int32)) % planes)
    wanted = sum(jnp.where(wanted == k, i, 0) for i, k in enumerate(order))
    for part in panels:
        while len(part) < planes:
            part.append(onward(part[-1]))

    kept, sent = off_parts(wanted, own, other, panels[0])
    blocks = [panel] + [jnp.concatenate([part[k] for part in panels], axis=1) for k in range(1, planes)]
    strips = [Strip(block) for block in sync(*blocks, sent)[:-1]]
    early, late = strips[:GATED], strips[GATED:]
    for strip in early:
        strip.hop()
    offs = [[kept + to_partner(sent)]]
    offs[0].append(onward(offs[0][0]))
    offs[0][1], *values = sync(offs[0][1], *(strip.come for strip in early))
    for strip, value in zip(early, values):
        strip.come = value
        strip.keep()
    for part in panels[1:]:
        kept, sent = off_parts(wanted, own, other, part)
        offs.append([kept + to_partner(sent)])
    for part in offs:
        while len(part) < planes:
            part.append(onward(part[-1]))
    turned = [strip.rest() for strip in strips]
    diag, gate = [], None
    for (start, _), part in zip(cuts, offs):
        if gate is not None:
            part[-1], _ = sync(part[-1], gate)
        kept, sent = diag_parts(member[None], inv_diag, start, turned, part)
        gate = sent
        diag.append(kept - to_partner(sent))
    return jnp.concatenate([part[0] for part in offs], axis=1), jnp.concatenate(diag, axis=1)


def solution(mesh):
    rows, cols = mesh.shape["row"], mesh.shape["col"]
    placed = (P("row", "col"), P("row", "col"), P("row"), P("row", "col"))
    return jax.shard_map(
        functools.partial(shards, rows // MEMBERS, cols),
        mesh=mesh,
        in_specs=placed,
        out_specs=(P("row", "col"), P("row", "col")),
        check_vma=False,
    )
```

```python
import functools

import jax
import jax.numpy as jnp
from jax import lax
from jax.experimental import pallas as pl
from jax.experimental.pallas import tpu as pltpu
from jax.sharding import PartitionSpec as P

MEMBERS = 2
CUT = 0.6
FIRST, NEAR, LAST, SKEW, SPLIT, ORDER = 'a', '', False, False, True, False
VMEM = 24
PICK, OFF, DIAG, TURN = 1, 1, 1, 1
PLAN = {(0, 1): ('k1a', 'y1a'), (1, 1): ('k1b', 'y2b'), (2, 1): ('k1a', 'y1a'), (3, 1): ('k1b', 'y2a'), (3, 2): ('y2b', 'y3a')}
BF16 = jnp.bfloat16
F32 = jnp.float32


def split(x):
    high = x.astype(BF16)
    return high, (x - high.astype(F32)).astype(BF16)


def dot(a, b):
    return jnp.dot(a, b, preferred_element_type=F32)


def dot3(a, b):
    return dot(a[0], b[0]) + (dot(a[0], b[1]) + dot(a[1], b[0]))


def whole(*shape):
    return pl.BlockSpec(shape, lambda *_: (0,) * len(shape))


def params():
    return pltpu.CompilerParams(vmem_limit_bytes=VMEM * 2**20)


def cost(scale, flops, moved):
    return pl.CostEstimate(flops=int(scale * flops), bytes_accessed=int(scale * moved), transcendentals=0)


def pick_kernel(rows_ref, member_ref, anc, own_ref, lists_ref, keep_ref, send_ref, picked, sem):
    count, width = picked.shape[0], picked.shape[1] // MEMBERS

    def fetch(i, carry):
        row = jnp.where(rows_ref[i] < 0, i, rows_ref[i])
        pltpu.make_async_copy(anc.at[pl.ds(row, 1), :], picked.at[pl.ds(i, 1), :], sem).start()
        return carry

    lax.fori_loop(0, count, fetch, 0, unroll=8)
    live = own_ref[...] >= 0
    ancestor = lax.broadcasted_iota(jnp.int32, (width, count), 0)
    chosen = [(ancestor == lists_ref[k : k + 1, :]).astype(BF16) for k in range(MEMBERS)]
    pltpu.make_async_copy(anc.at[pl.ds(0, count), :], picked, sem).wait()
    for k, out in enumerate((keep_ref, send_ref)):
        member = jnp.bitwise_xor(member_ref[0], k)
        high, low = split(picked[:, pl.ds(pl.multiple_of(member * width, 128), width)])
        out[...] = jnp.where(live, dot(high, chosen[k]) + dot(low, chosen[k]), 0.0)


def pick(anc, rows, member, lists):
    count, width = rows.shape[0], anc.shape[1]
    square = jax.ShapeDtypeStruct((count, count), F32)
    return pl.pallas_call(
        pick_kernel,
        grid_spec=pltpu.PrefetchScalarGridSpec(
            num_scalar_prefetch=2,
            grid=(1,),
            in_specs=[pl.BlockSpec(memory_space=pl.ANY), whole(count, 1), whole(MEMBERS, count)],
            out_specs=[whole(count, count)] * 2,
            scratch_shapes=[pltpu.VMEM((count, width), F32), pltpu.SemaphoreType.DMA],
        ),
        out_shape=(square, square),
        compiler_params=params(),
        cost_estimate=cost(PICK, 4 * count * count * width, 16 * count * width),
        name="pick_compact",
    )(rows, member, anc, rows[:, None], lists)


def off_kernel(count, order_ref, *refs):
    own, other, blocks, (own_ref, other_ref) = refs[:count], refs[count : 2 * count], refs[2 * count : -2], refs[-2:]
    rows = own_ref.shape[0]
    total = None
    for step, block in enumerate(blocks):
        piece = jnp.concatenate([own[0][...], other[0][...]])
        for k in range(1, count):
            piece = jnp.where(order_ref[step] == k, jnp.concatenate([own[k][...], other[k][...]]), piece)
        term = dot3(split(piece), split(block[...]))
        total = term if total is None else total + term
    own_ref[...] = -total[:rows]
    other_ref[...] = -total[rows:]


def off_parts(order, own, other, blocks):
    count, width = blocks[0].shape
    out = jax.ShapeDtypeStruct((count, width), F32)
    return pl.pallas_call(
        functools.partial(off_kernel, len(own)),
        grid_spec=pltpu.PrefetchScalarGridSpec(
            num_scalar_prefetch=1,
            grid=(1,),
            in_specs=[whole(*x.shape) for x in (*own, *other, *blocks)],
            out_specs=[whole(count, width)] * 2,
        ),
        out_shape=(out, out),
        compiler_params=params(),
        cost_estimate=cost(OFF, 12 * count * count * width * len(blocks), 8 * count * count * len(blocks)),
        name="off_parts",
    )(order, *own, *other, *blocks)


def turn_kernel(flag_ref, held, come, high_ref, low_ref):
    strip = jnp.where(flag_ref[0] > 0, held[...], come[...]).T
    high_ref[...], low_ref[...] = split(strip)


def turn(flag, held, come):
    count, width = held.shape
    out = jax.ShapeDtypeStruct((width, count), BF16)
    return pl.pallas_call(
        turn_kernel,
        grid_spec=pltpu.PrefetchScalarGridSpec(
            num_scalar_prefetch=1,
            grid=(1,),
            in_specs=[whole(count, width)] * 2,
            out_specs=[whole(width, count)] * 2,
        ),
        out_shape=(out, out),
        compiler_params=params(),
        cost_estimate=cost(TURN, 0, 12 * count * width),
        name="turn_strip",
    )(flag, held, come)


def diag_kernel(start, member_ref, base_ref, *refs):
    count = (len(refs) - 3) // 3
    highs, lows, blocks = refs[:count], refs[count : 2 * count], refs[2 * count : -3]
    own_ref, other_ref, total = refs[-3:]
    half, width = own_ref.shape
    for step in range(count):
        term = dot3((highs[step][...], lows[step][...]), split(blocks[step][...]))
        total[...] = term if step == 0 else total[...] + term
    mine = pl.multiple_of(member_ref[0] * half, 8)
    own_ref[...] = base_ref[:, start : start + width] - total[pl.ds(mine, half), :]
    other_ref[...] = total[pl.ds(pl.multiple_of(half - mine, 8), half), :]


def diag_parts(member, base, start, strips, blocks):
    (strip_width, count), width = strips[0][0].shape, blocks[0].shape[1]
    half = strip_width // MEMBERS
    flat = [base, *(high for high, _ in strips), *(low for _, low in strips), *blocks]
    out = jax.ShapeDtypeStruct((half, width), F32)
    return pl.pallas_call(
        functools.partial(diag_kernel, start),
        grid_spec=pltpu.PrefetchScalarGridSpec(
            num_scalar_prefetch=1,
            grid=(1,),
            in_specs=[whole(*x.shape) for x in flat],
            out_specs=[whole(half, width)] * 2,
            scratch_shapes=[pltpu.VMEM((strip_width, width), F32)],
        ),
        out_shape=(out, out),
        compiler_params=params(),
        cost_estimate=cost(DIAG, 6 * count * strip_width * width * len(blocks), 4 * count * strip_width * len(blocks)),
        name="diag_parts",
    )(member, *flat)


def diag_first_kernel(*refs):
    count, total = len(refs) // 3, refs[-1]
    for step in range(count):
        high, low, block = refs[step::count][:3]
        term = dot3((high[...], low[...]), split(block[...]))
        total[...] = term if step == 0 else total[...] + term


def diag_first(strips, blocks):
    (strip_width, count), width = strips[0][0].shape, blocks[0].shape[1]
    flat = [*(high for high, _ in strips), *(low for _, low in strips), *blocks]
    return pl.pallas_call(
        diag_first_kernel,
        grid=(1,),
        in_specs=[whole(*x.shape) for x in flat],
        out_specs=whole(strip_width, width),
        out_shape=jax.ShapeDtypeStruct((strip_width, width), F32),
        compiler_params=params(),
        cost_estimate=cost(DIAG, 6 * count * strip_width * width * len(blocks), 4 * count * strip_width * len(blocks)),
        name="diag_first",
    )(*flat)


def diag_last_kernel(start, member_ref, first, base_ref, high, low, block, own_ref, other_ref, total):
    half, width = own_ref.shape
    total[...] = first[...] + dot3((high[...], low[...]), split(block[...]))
    mine = pl.multiple_of(member_ref[0] * half, 8)
    own_ref[...] = base_ref[:, start : start + width] - total[pl.ds(mine, half), :]
    other_ref[...] = total[pl.ds(pl.multiple_of(half - mine, 8), half), :]


def diag_last(member, first, base, start, strip, block):
    (strip_width, count), width = strip[0].shape, block.shape[1]
    half = strip_width // MEMBERS
    out = jax.ShapeDtypeStruct((half, width), F32)
    return pl.pallas_call(
        functools.partial(diag_last_kernel, start),
        grid_spec=pltpu.PrefetchScalarGridSpec(
            num_scalar_prefetch=1,
            grid=(1,),
            in_specs=[whole(*x.shape) for x in (first, base, *strip, block)],
            out_specs=[whole(half, width)] * 2,
            scratch_shapes=[pltpu.VMEM((strip_width, width), F32)],
        ),
        out_shape=(out, out),
        compiler_params=params(),
        cost_estimate=cost(DIAG, 6 * count * strip_width * width, 8 * count * strip_width),
        name="diag_last",
    )(member, first, base, *strip, block)


def shards(planes, cols, anc_inverse, panel, local_rows, inv_diag):
    axes = ("row", "col")
    row, col = lax.axis_index("row"), lax.axis_index("col")
    plane, member = row // MEMBERS, row % MEMBERS
    grid = [(z, y, c) for z in range(planes) for y in range(MEMBERS) for c in range(cols)]

    def place(z, y, c):
        return (z * MEMBERS + y) * cols + c

    def move(x, target, some=lambda z, y, c: True):
        return lax.ppermute(x, axes, [(place(*d), place(*target(*d))) for d in grid if some(*d)])

    def to_partner(x):
        return move(x, lambda z, y, c: (z, 1 - y, c))

    def onward(x):
        return move(x, lambda z, y, c: ((z + 1) % planes, y, c))

    def sync(*values):
        return list(lax.optimization_barrier(values))

    class Strip:
        def __init__(self, block):
            self.block, self.holders, self.apart, self.made = block, [0], cols // 2, 0

        def hop(self):
            apart, holders = self.apart, self.holders
            self.made += 1
            self.come = move(self.block, lambda z, y, c: (z, y, c ^ apart), lambda z, y, c: (c ^ z) in holders)

        def has(self):
            return functools.reduce(jnp.logical_or, [(col ^ plane) == h for h in self.holders])

        def keep(self):
            self.block = jnp.where(self.has(), self.block, self.come)
            self.holders = self.holders + [h ^ self.apart for h in self.holders]
            self.apart //= 2
            self.come = None

        def finish(self):
            if not self.made:
                self.hop()
            while self.apart > 1:
                self.keep()
                self.hop()
            return turn(self.has().astype(jnp.int32)[None], self.block, self.come)

    width = panel.shape[1]
    cut = max(1, round(CUT * width / 128)) * 128
    cuts = [(0, cut), (cut, width)] if cut < width else [(0, width)]
    def at(event, value):
        nonlocal strips
        due = [k for (k, hop), (_, hold) in PLAN.items() if hold == event and k < len(strips) and strips[k].made == hop]
        if due:
            value, *comes = sync(value, *(strips[k].come for k in due))
            for k, come in zip(due, comes):
                strips[k].come = come
        for (k, hop), (start, _) in PLAN.items():
            if start == event and k < planes:
                while len(strips) <= k:
                    strips.append(Strip(joined_panel(len(strips))))
                if hop == 2:
                    strips[k].keep()
                if event != "begin":
                    strips[k].block, _ = sync(strips[k].block, value)
                strips[k].hop()
        return value

    def joined_panel(k):
        return jnp.concatenate([part[k] for part in panels], axis=1) if k else panel

    strips = []
    at("begin", None)
    panels = [[panel[:, a:b]] for a, b in cuts]
    for part in panels:
        part.append(onward(part[0]))
    lists = jnp.stack([move(local_rows, lambda z, y, c: (c, y, z)), move(local_rows, lambda z, y, c: (c, 1 - y, z))])
    keep, send = pick(anc_inverse, local_rows, member[None], lists)
    if FIRST == "a":
        send, panels[0][1] = sync(send, panels[0][1])
    elif FIRST == "ab":
        send, *firsts = sync(send, *(part[1] for part in panels))
        for part, value in zip(panels, firsts):
            part[1] = value
    send = at("pick", send)
    apart, order = cols // 2, [0, cols // 2]
    own = [keep, move(keep, lambda z, y, c: (z, y, c ^ apart))]
    other = [to_partner(send), move(send, lambda z, y, c: (z, 1 - y, c ^ apart))]
    for k, part in enumerate(panels):
        part.append(onward(part[1]))
        if NEAR == "ab"[k]:
            part[2], own[1], *other = sync(part[2], own[1], *other)
        part[2] = at("ab"[k] + "2", part[2])
    while apart > 1:
        apart //= 2
        for held in (own, other):
            held += [move(piece, lambda z, y, c: (z, y, c ^ apart)) for piece in held]
        order = order + [k ^ apart for k in order]
    wanted = col ^ ((plane - jnp.arange(planes, dtype=jnp.int32)) % planes)
    wanted = sum(jnp.where(wanted == k, i, 0) for i, k in enumerate(order))
    for k, part in enumerate(panels):
        while len(part) < planes:
            part.append(onward(part[-1]))
        part[-1] = at("ab"[k] + "3", part[-1])

    kept, sent = off_parts(wanted, own, other, panels[0])
    sent = at("k1a", sent)
    value = kept + to_partner(sent)
    if LAST and len(panels) > 1:
        value, panels[1][-1] = sync(value, panels[1][-1])
    offs = [[at("xa", value)]]
    offs[0].append(at("y1a", onward(offs[0][0])))
    for part in panels[1:]:
        kept, sent = off_parts(wanted, own, other, part)
        sent = at("k1b", sent)
        value = kept + to_partner(sent)
        if SKEW:
            value, offs[0][1] = sync(value, offs[0][1])
        offs.append([at("xb", value)])
        offs[-1].append(at("y1b", onward(offs[-1][0])))
    for step in range(2, planes):
        for k, part in enumerate(offs):
            part.append(at(f"y{step}" + "ab"[k], onward(part[-1])))
    while len(strips) < planes:
        strips.append(Strip(joined_panel(len(strips))))
    turned = [strip.finish() for strip in strips]
    diag, gate = [], None
    for (start, _), part in zip(cuts, offs):
        if gate is not None:
            part[-1], _ = sync(part[-1], gate)
        if SPLIT:
            total = diag_first(turned[:-1], part[:-1])
            kept, sent = diag_last(member[None], total, inv_diag, start, turned[-1], part[-1])
        else:
            kept, sent = diag_parts(member[None], inv_diag, start, turned, part)
        if ORDER:
            gate = sent
        diag.append(kept - to_partner(sent))
    return jnp.concatenate([part[0] for part in offs], axis=1), jnp.concatenate(diag, axis=1)


def solution(mesh):
    rows, cols = mesh.shape["row"], mesh.shape["col"]
    placed = (P("row", "col"), P("row", "col"), P("row"), P("row", "col"))
    return jax.shard_map(
        functools.partial(shards, rows // MEMBERS, cols),
        mesh=mesh,
        in_specs=placed,
        out_specs=(P("row", "col"), P("row", "col")),
        check_vma=False,
    )
```

```python
import functools

import jax
import jax.numpy as jnp
from jax import lax
from jax.experimental import pallas as pl
from jax.experimental.pallas import tpu as pltpu
from jax.sharding import PartitionSpec as P

MEMBERS = 2
CUT = 0.6
PLAN = {
    (0, 1): ("k1a", "y1a"),
    (1, 1): ("k1b", "y2b"),
    (2, 1): ("k1a", "y1a"),
    (3, 1): ("y1a", None),
    (3, 2): ("y2b", "y3a"),
}
BF16 = jnp.bfloat16
F32 = jnp.float32


def split(x):
    limit = float(jnp.finfo(BF16).max)
    high = jnp.clip(x, -limit, limit).astype(BF16)
    return high, (x - high.astype(F32)).astype(BF16)


def dot(a, b):
    return jnp.dot(a, b, preferred_element_type=F32)


def dot3(a, b):
    return dot(a[0], b[0]) + (dot(a[0], b[1]) + dot(a[1], b[0]))


def whole(*shape):
    return pl.BlockSpec(shape, lambda *_: (0,) * len(shape))


def params():
    return pltpu.CompilerParams(vmem_limit_bytes=24 * 2**20)


def cost(flops, moved):
    return pl.CostEstimate(flops=flops, bytes_accessed=moved, transcendentals=0)


def pick_kernel(rows_ref, member_ref, anc, own_ref, lists_ref, keep_ref, send_ref, picked, sem):
    count, width = picked.shape[0], picked.shape[1] // MEMBERS

    def fetch(i, carry):
        row = jnp.where(rows_ref[i] < 0, i, rows_ref[i])
        pltpu.make_async_copy(anc.at[pl.ds(row, 1), :], picked.at[pl.ds(i, 1), :], sem).start()
        return carry

    lax.fori_loop(0, count, fetch, 0, unroll=8)
    live = own_ref[...] >= 0
    ancestor = lax.broadcasted_iota(jnp.int32, (width, count), 0)
    chosen = [(ancestor == lists_ref[k : k + 1, :]).astype(BF16) for k in range(MEMBERS)]
    pltpu.make_async_copy(anc.at[pl.ds(0, count), :], picked, sem).wait()
    for k, out in enumerate((keep_ref, send_ref)):
        member = jnp.bitwise_xor(member_ref[0], k)
        high, low = split(picked[:, pl.ds(pl.multiple_of(member * width, 128), width)])
        out[...] = jnp.where(live, dot(high, chosen[k]) + dot(low, chosen[k]), 0.0)


def pick(anc, rows, member, lists):
    count, width = rows.shape[0], anc.shape[1]
    square = jax.ShapeDtypeStruct((count, count), F32)
    return pl.pallas_call(
        pick_kernel,
        grid_spec=pltpu.PrefetchScalarGridSpec(
            num_scalar_prefetch=2,
            grid=(1,),
            in_specs=[pl.BlockSpec(memory_space=pl.ANY), whole(count, 1), whole(MEMBERS, count)],
            out_specs=[whole(count, count)] * 2,
            scratch_shapes=[pltpu.VMEM((count, width), F32), pltpu.SemaphoreType.DMA],
        ),
        out_shape=(square, square),
        compiler_params=params(),
        cost_estimate=cost(4 * count * count * width, 16 * count * width),
        name="pick_compact",
    )(rows, member, anc, rows[:, None], lists)


def pack_kernel(count, order_ref, *refs):
    own, other, (high_ref, low_ref) = refs[:count], refs[count : 2 * count], refs[2 * count :]
    for step in range(high_ref.shape[0]):
        for k in range(count):

            @pl.when(order_ref[step] == k)
            def _():
                piece = jnp.concatenate([own[k][...], other[k][...]])
                high_ref[step], low_ref[step] = split(piece)


def pack(order, own, other):
    count, steps = own[0].shape[0], order.shape[0]
    out = jax.ShapeDtypeStruct((steps, 2 * count, count), BF16)
    return pl.pallas_call(
        functools.partial(pack_kernel, len(own)),
        grid_spec=pltpu.PrefetchScalarGridSpec(
            num_scalar_prefetch=1,
            grid=(1,),
            in_specs=[whole(count, count)] * (2 * len(own)),
            out_specs=[whole(*out.shape)] * 2,
        ),
        out_shape=(out, out),
        compiler_params=params(),
        cost_estimate=cost(0, 16 * count * count * steps),
        name="pack_pieces",
    )(order, *own, *other)


def off_kernel(high, low, *refs):
    blocks, (own_ref, other_ref) = refs[:-2], refs[-2:]
    rows = own_ref.shape[0]
    total = None
    for step, block in enumerate(blocks):
        term = dot3((high[step], low[step]), split(block[...]))
        total = term if total is None else total + term
    own_ref[...] = -total[:rows]
    other_ref[...] = -total[rows:]


def off_parts(pieces, blocks):
    count, width = blocks[0].shape
    out = jax.ShapeDtypeStruct((count, width), F32)
    return pl.pallas_call(
        off_kernel,
        grid=(1,),
        in_specs=[whole(*x.shape) for x in (*pieces, *blocks)],
        out_specs=[whole(count, width)] * 2,
        out_shape=(out, out),
        compiler_params=params(),
        cost_estimate=cost(12 * count * count * width * len(blocks), 8 * count * count * len(blocks)),
        name="off_parts",
    )(*pieces, *blocks)


def turn_kernel(flag_ref, held, come, high_ref, low_ref):
    strip = jnp.where(flag_ref[0] > 0, held[...], come[...]).T
    high_ref[...], low_ref[...] = split(strip)


def turn(flag, held, come):
    count, width = held.shape
    out = jax.ShapeDtypeStruct((width, count), BF16)
    return pl.pallas_call(
        turn_kernel,
        grid_spec=pltpu.PrefetchScalarGridSpec(
            num_scalar_prefetch=1,
            grid=(1,),
            in_specs=[whole(count, width)] * 2,
            out_specs=[whole(width, count)] * 2,
        ),
        out_shape=(out, out),
        compiler_params=params(),
        cost_estimate=cost(0, 12 * count * width),
        name="turn_strip",
    )(flag, held, come)


def diag_first_kernel(*refs):
    count, total = len(refs) // 3, refs[-1]
    for step in range(count):
        high, low, block = refs[step::count][:3]
        term = dot3((high[...], low[...]), split(block[...]))
        total[...] = term if step == 0 else total[...] + term


def diag_first(strips, blocks):
    (strip_width, count), width = strips[0][0].shape, blocks[0].shape[1]
    flat = [*(high for high, _ in strips), *(low for _, low in strips), *blocks]
    return pl.pallas_call(
        diag_first_kernel,
        grid=(1,),
        in_specs=[whole(*x.shape) for x in flat],
        out_specs=whole(strip_width, width),
        out_shape=jax.ShapeDtypeStruct((strip_width, width), F32),
        compiler_params=params(),
        cost_estimate=cost(6 * count * strip_width * width * len(blocks), 4 * count * strip_width * len(blocks)),
        name="diag_first",
    )(*flat)


def diag_last_kernel(start, member_ref, first, base_ref, high, low, block, own_ref, other_ref, total):
    half, width = own_ref.shape
    total[...] = first[...] + dot3((high[...], low[...]), split(block[...]))
    mine = pl.multiple_of(member_ref[0] * half, 8)
    own_ref[...] = base_ref[:, start : start + width] - total[pl.ds(mine, half), :]
    other_ref[...] = total[pl.ds(pl.multiple_of(half - mine, 8), half), :]


def diag_last(member, first, base, start, strip, block):
    (strip_width, count), width = strip[0].shape, block.shape[1]
    half = strip_width // MEMBERS
    out = jax.ShapeDtypeStruct((half, width), F32)
    return pl.pallas_call(
        functools.partial(diag_last_kernel, start),
        grid_spec=pltpu.PrefetchScalarGridSpec(
            num_scalar_prefetch=1,
            grid=(1,),
            in_specs=[whole(*x.shape) for x in (first, base, *strip, block)],
            out_specs=[whole(half, width)] * 2,
            scratch_shapes=[pltpu.VMEM((strip_width, width), F32)],
        ),
        out_shape=(out, out),
        compiler_params=params(),
        cost_estimate=cost(6 * count * strip_width * width, 8 * count * strip_width),
        name="diag_last",
    )(member, first, base, *strip, block)


def shards(planes, cols, anc_inverse, panel, local_rows, inv_diag):
    axes = ("row", "col")
    row, col = lax.axis_index("row"), lax.axis_index("col")
    plane, member = row // MEMBERS, row % MEMBERS
    grid = [(z, y, c) for z in range(planes) for y in range(MEMBERS) for c in range(cols)]

    def place(z, y, c):
        return (z * MEMBERS + y) * cols + c

    def move(x, target, some=lambda z, y, c: True):
        return lax.ppermute(x, axes, [(place(*d), place(*target(*d))) for d in grid if some(*d)])

    def to_partner(x):
        return move(x, lambda z, y, c: (z, 1 - y, c))

    def onward(x):
        return move(x, lambda z, y, c: ((z + 1) % planes, y, c))

    def sync(*values):
        return list(lax.optimization_barrier(values))

    class Strip:
        def __init__(self, block):
            self.block, self.holders, self.apart, self.made = block, [0], cols // 2, 0

        def hop(self):
            apart, holders = self.apart, self.holders
            self.made += 1
            self.come = move(self.block, lambda z, y, c: (z, y, c ^ apart), lambda z, y, c: (c ^ z) in holders)

        def has(self):
            return functools.reduce(jnp.logical_or, [(col ^ plane) == h for h in self.holders])

        def keep(self):
            self.block = jnp.where(self.has(), self.block, self.come)
            self.holders = self.holders + [h ^ self.apart for h in self.holders]
            self.apart //= 2
            self.come = None

        def finish(self):
            if not self.made:
                self.hop()
            while self.apart > 1:
                self.keep()
                self.hop()
            return turn(self.has().astype(jnp.int32)[None], self.block, self.come)

    width = panel.shape[1]
    cut = max(1, round(CUT * width / 128)) * 128
    cuts = [(0, cut), (cut, width)] if cut < width else [(0, width)]

    def at(event, value):
        due = [k for (k, hop), (_, hold) in PLAN.items() if hold == event and k < len(strips) and strips[k].made == hop]
        if due:
            value, *comes = sync(value, *(strips[k].come for k in due))
            for k, come in zip(due, comes):
                strips[k].come = come
        for (k, hop), (start, _) in PLAN.items():
            if start == event and k < planes:
                while len(strips) <= k:
                    strips.append(Strip(joined_panel(len(strips))))
                if hop == 2:
                    strips[k].keep()
                strips[k].block, _ = sync(strips[k].block, value)
                strips[k].hop()
        return value

    def joined_panel(k):
        return jnp.concatenate([part[k] for part in panels], axis=1) if k else panel

    strips = []
    panels = [[panel[:, a:b]] for a, b in cuts]
    for part in panels:
        part.append(onward(part[0]))
    lists = jnp.stack([move(local_rows, lambda z, y, c: (c, y, z)), move(local_rows, lambda z, y, c: (c, 1 - y, z))])
    keep, send = pick(anc_inverse, local_rows, member[None], lists)
    send, panels[0][1] = sync(send, panels[0][1])
    apart, order = cols // 2, [0, cols // 2]
    own = [keep, move(keep, lambda z, y, c: (z, y, c ^ apart))]
    other = [to_partner(send), move(send, lambda z, y, c: (z, 1 - y, c ^ apart))]
    for part in panels:
        part.append(onward(part[1]))
    while apart > 1:
        apart //= 2
        for held in (own, other):
            held += [move(piece, lambda z, y, c: (z, y, c ^ apart)) for piece in held]
        order = order + [k ^ apart for k in order]
    wanted = col ^ ((plane - jnp.arange(planes, dtype=jnp.int32)) % planes)
    wanted = sum(jnp.where(wanted == k, i, 0) for i, k in enumerate(order))
    for k, part in enumerate(panels):
        if k:
            part[2], panels[0][3] = sync(part[2], panels[0][3])
        while len(part) < planes:
            part.append(onward(part[-1]))

    pieces = pack(wanted, own, other)
    offs = []
    for k, part in enumerate(panels):
        kept, sent = off_parts(pieces, part)
        sent = at("k1" + "ab"[k], sent)
        offs.append([kept + to_partner(sent)])
    for step in range(1, planes):
        for k, part in enumerate(offs):
            part.append(at(f"y{step}" + "ab"[k], onward(part[-1])))
    while len(strips) < planes:
        strips.append(Strip(joined_panel(len(strips))))
    turned = [strip.finish() for strip in strips]
    diag = []
    for (start, _), part in zip(cuts, offs):
        total = diag_first(turned[:-1], part[:-1])
        kept, sent = diag_last(member[None], total, inv_diag, start, turned[-1], part[-1])
        diag.append(kept - to_partner(sent))
    return jnp.concatenate([part[0] for part in offs], axis=1), jnp.concatenate(diag, axis=1)


def solution(mesh):
    rows, cols = mesh.shape["row"], mesh.shape["col"]
    placed = (P("row", "col"), P("row", "col"), P("row"), P("row", "col"))
    return jax.shard_map(
        functools.partial(shards, rows // MEMBERS, cols),
        mesh=mesh,
        in_specs=placed,
        out_specs=(P("row", "col"), P("row", "col")),
        check_vma=False,
    )
```

```python
import functools

import jax
import jax.numpy as jnp
from jax import lax
from jax.experimental import pallas as pl
from jax.experimental.pallas import tpu as pltpu
from jax.sharding import PartitionSpec as P

MEMBERS = 2
CUT = 0.6
PLAN = {
    (0, 1): ("k1a", "y1a"),
    (1, 1): ("k1b", "y2b"),
    (2, 1): ("k1a", "y1a"),
    (3, 1): ("y1a", None),
    (3, 2): ("y2b", "y3a"),
}
BF16 = jnp.bfloat16
F32 = jnp.float32


def split(x):
    limit = float(jnp.finfo(BF16).max)
    high = jnp.clip(x, -limit, limit).astype(BF16)
    return high, (x - high.astype(F32)).astype(BF16)


def dot(a, b):
    return jnp.dot(a, b, preferred_element_type=F32)


def dot3(a, b):
    return dot(a[0], b[0]) + (dot(a[0], b[1]) + dot(a[1], b[0]))


def whole(*shape):
    return pl.BlockSpec(shape, lambda *_: (0,) * len(shape))


def params():
    return pltpu.CompilerParams(vmem_limit_bytes=24 * 2**20)


def cost(flops, moved):
    return pl.CostEstimate(flops=flops, bytes_accessed=moved, transcendentals=0)


def pick_kernel(rows_ref, member_ref, anc, own_ref, lists_ref, keep_ref, send_ref, picked, sem):
    count, width = picked.shape[0], picked.shape[1] // MEMBERS

    def fetch(i, carry):
        row = jnp.where(rows_ref[i] < 0, i, rows_ref[i])
        pltpu.make_async_copy(anc.at[pl.ds(row, 1), :], picked.at[pl.ds(i, 1), :], sem).start()
        return carry

    lax.fori_loop(0, count, fetch, 0, unroll=8)
    live = own_ref[...] >= 0
    ancestor = lax.broadcasted_iota(jnp.int32, (width, count), 0)
    chosen = [(ancestor == lists_ref[k : k + 1, :]).astype(BF16) for k in range(MEMBERS)]
    pltpu.make_async_copy(anc.at[pl.ds(0, count), :], picked, sem).wait()
    for k, out in enumerate((keep_ref, send_ref)):
        member = jnp.bitwise_xor(member_ref[0], k)
        high, low = split(picked[:, pl.ds(pl.multiple_of(member * width, 128), width)])
        out[...] = jnp.where(live, dot(high, chosen[k]) + dot(low, chosen[k]), 0.0)


def pick(anc, rows, member, lists):
    count, width = rows.shape[0], anc.shape[1]
    square = jax.ShapeDtypeStruct((count, count), F32)
    return pl.pallas_call(
        pick_kernel,
        grid_spec=pltpu.PrefetchScalarGridSpec(
            num_scalar_prefetch=2,
            grid=(1,),
            in_specs=[pl.BlockSpec(memory_space=pl.ANY), whole(count, 1), whole(MEMBERS, count)],
            out_specs=[whole(count, count)] * 2,
            scratch_shapes=[pltpu.VMEM((count, width), F32), pltpu.SemaphoreType.DMA],
        ),
        out_shape=(square, square),
        compiler_params=params(),
        cost_estimate=cost(4 * count * count * width, 16 * count * width),
        name="pick_compact",
    )(rows, member, anc, rows[:, None], lists)


def pack_kernel(count, order_ref, *refs):
    own, other, (high_ref, low_ref) = refs[:count], refs[count : 2 * count], refs[2 * count :]
    for step in range(high_ref.shape[0]):
        for k in range(count):

            @pl.when(order_ref[step] == k)
            def _():
                piece = jnp.concatenate([own[k][...], other[k][...]])
                high_ref[step], low_ref[step] = split(piece)


def pack(order, own, other):
    count, steps = own[0].shape[0], order.shape[0]
    out = jax.ShapeDtypeStruct((steps, 2 * count, count), BF16)
    return pl.pallas_call(
        functools.partial(pack_kernel, len(own)),
        grid_spec=pltpu.PrefetchScalarGridSpec(
            num_scalar_prefetch=1,
            grid=(1,),
            in_specs=[whole(count, count)] * (2 * len(own)),
            out_specs=[whole(*out.shape)] * 2,
        ),
        out_shape=(out, out),
        compiler_params=params(),
        cost_estimate=cost(0, 16 * count * count * steps),
        name="pack_pieces",
    )(order, *own, *other)


def off_kernel(high, low, *refs):
    blocks, (own_ref, other_ref) = refs[:-2], refs[-2:]
    rows = own_ref.shape[0]
    total = None
    for step, block in enumerate(blocks):
        term = dot3((high[step], low[step]), split(block[...]))
        total = term if total is None else total + term
    own_ref[...] = -total[:rows]
    other_ref[...] = -total[rows:]


def off_parts(pieces, blocks):
    count, width = blocks[0].shape
    out = jax.ShapeDtypeStruct((count, width), F32)
    return pl.pallas_call(
        off_kernel,
        grid=(1,),
        in_specs=[whole(*x.shape) for x in (*pieces, *blocks)],
        out_specs=[whole(count, width)] * 2,
        out_shape=(out, out),
        compiler_params=params(),
        cost_estimate=cost(12 * count * count * width * len(blocks), 8 * count * count * len(blocks)),
        name="off_parts",
    )(*pieces, *blocks)


def turn_kernel(flag_ref, held, come, high_ref, low_ref):
    strip = jnp.where(flag_ref[0] > 0, held[...], come[...]).T
    high_ref[...], low_ref[...] = split(strip)


def turn(flag, held, come):
    count, width = held.shape
    out = jax.ShapeDtypeStruct((width, count), BF16)
    return pl.pallas_call(
        turn_kernel,
        grid_spec=pltpu.PrefetchScalarGridSpec(
            num_scalar_prefetch=1,
            grid=(1,),
            in_specs=[whole(count, width)] * 2,
            out_specs=[whole(width, count)] * 2,
        ),
        out_shape=(out, out),
        compiler_params=params(),
        cost_estimate=cost(0, 12 * count * width),
        name="turn_strip",
    )(flag, held, come)


def diag_first_kernel(*refs):
    count, total = len(refs) // 3, refs[-1]
    for step in range(count):
        high, low, block = refs[step::count][:3]
        term = dot3((high[...], low[...]), split(block[...]))
        total[...] = term if step == 0 else total[...] + term


def diag_first(strips, blocks):
    (strip_width, count), width = strips[0][0].shape, blocks[0].shape[1]
    flat = [*(high for high, _ in strips), *(low for _, low in strips), *blocks]
    return pl.pallas_call(
        diag_first_kernel,
        grid=(1,),
        in_specs=[whole(*x.shape) for x in flat],
        out_specs=whole(strip_width, width),
        out_shape=jax.ShapeDtypeStruct((strip_width, width), F32),
        compiler_params=params(),
        cost_estimate=cost(6 * count * strip_width * width * len(blocks) // 10, 4 * count * strip_width * len(blocks) // 10),
        name="diag_first",
    )(*flat)


def diag_last_kernel(start, member_ref, first, base_ref, high, low, block, own_ref, other_ref, total):
    half, width = own_ref.shape
    total[...] = first[...] + dot3((high[...], low[...]), split(block[...]))
    mine = pl.multiple_of(member_ref[0] * half, 8)
    own_ref[...] = base_ref[:, start : start + width] - total[pl.ds(mine, half), :]
    other_ref[...] = total[pl.ds(pl.multiple_of(half - mine, 8), half), :]


def diag_last(member, first, base, start, strip, block):
    (strip_width, count), width = strip[0].shape, block.shape[1]
    half = strip_width // MEMBERS
    out = jax.ShapeDtypeStruct((half, width), F32)
    return pl.pallas_call(
        functools.partial(diag_last_kernel, start),
        grid_spec=pltpu.PrefetchScalarGridSpec(
            num_scalar_prefetch=1,
            grid=(1,),
            in_specs=[whole(*x.shape) for x in (first, base, *strip, block)],
            out_specs=[whole(half, width)] * 2,
            scratch_shapes=[pltpu.VMEM((strip_width, width), F32)],
        ),
        out_shape=(out, out),
        compiler_params=params(),
        cost_estimate=cost(6 * count * strip_width * width // 10, 8 * count * strip_width // 10),
        name="diag_last",
    )(member, first, base, *strip, block)


def shards(planes, cols, anc_inverse, panel, local_rows, inv_diag):
    axes = ("row", "col")
    row, col = lax.axis_index("row"), lax.axis_index("col")
    plane, member = row // MEMBERS, row % MEMBERS
    grid = [(z, y, c) for z in range(planes) for y in range(MEMBERS) for c in range(cols)]

    def place(z, y, c):
        return (z * MEMBERS + y) * cols + c

    def move(x, target, some=lambda z, y, c: True):
        return lax.ppermute(x, axes, [(place(*d), place(*target(*d))) for d in grid if some(*d)])

    def to_partner(x):
        return move(x, lambda z, y, c: (z, 1 - y, c))

    def onward(x):
        return move(x, lambda z, y, c: ((z + 1) % planes, y, c))

    def sync(*values):
        return list(lax.optimization_barrier(values))

    class Strip:
        def __init__(self, block):
            self.block, self.holders, self.apart, self.made = block, [0], cols // 2, 0

        def hop(self):
            apart, holders = self.apart, self.holders
            self.made += 1
            self.come = move(self.block, lambda z, y, c: (z, y, c ^ apart), lambda z, y, c: (c ^ z) in holders)

        def has(self):
            return functools.reduce(jnp.logical_or, [(col ^ plane) == h for h in self.holders])

        def keep(self):
            self.block = jnp.where(self.has(), self.block, self.come)
            self.holders = self.holders + [h ^ self.apart for h in self.holders]
            self.apart //= 2
            self.come = None

        def finish(self):
            if not self.made:
                self.hop()
            while self.apart > 1:
                self.keep()
                self.hop()
            return turn(self.has().astype(jnp.int32)[None], self.block, self.come)

    width = panel.shape[1]
    cut = max(1, round(CUT * width / 128)) * 128
    cuts = [(0, cut), (cut, width)] if cut < width else [(0, width)]

    def at(event, value):
        due = [k for (k, hop), (_, hold) in PLAN.items() if hold == event and k < len(strips) and strips[k].made == hop]
        if due:
            value, *comes = sync(value, *(strips[k].come for k in due))
            for k, come in zip(due, comes):
                strips[k].come = come
        for (k, hop), (start, _) in PLAN.items():
            if start == event and k < planes:
                while len(strips) <= k:
                    strips.append(Strip(joined_panel(len(strips))))
                if hop == 2:
                    strips[k].keep()
                strips[k].block, _ = sync(strips[k].block, value)
                strips[k].hop()
        return value

    def joined_panel(k):
        return jnp.concatenate([part[k] for part in panels], axis=1) if k else panel

    strips = []
    panels = [[panel[:, a:b]] for a, b in cuts]
    for part in panels:
        part.append(onward(part[0]))
    lists = jnp.stack([move(local_rows, lambda z, y, c: (c, y, z)), move(local_rows, lambda z, y, c: (c, 1 - y, z))])
    keep, send = pick(anc_inverse, local_rows, member[None], lists)
    send, panels[0][1] = sync(send, panels[0][1])
    apart, order = cols // 2, [0, cols // 2]
    own = [keep, move(keep, lambda z, y, c: (z, y, c ^ apart))]
    other = [to_partner(send), move(send, lambda z, y, c: (z, 1 - y, c ^ apart))]
    for part in panels:
        part.append(onward(part[1]))
    while apart > 1:
        apart //= 2
        for held in (own, other):
            held += [move(piece, lambda z, y, c: (z, y, c ^ apart)) for piece in held]
        order = order + [k ^ apart for k in order]
    wanted = col ^ ((plane - jnp.arange(planes, dtype=jnp.int32)) % planes)
    wanted = sum(jnp.where(wanted == k, i, 0) for i, k in enumerate(order))
    for k, part in enumerate(panels):
        if k:
            part[2], panels[0][3] = sync(part[2], panels[0][3])
        while len(part) < planes:
            part.append(onward(part[-1]))

    pieces = pack(wanted, own, other)
    offs = []
    for k, part in enumerate(panels):
        kept, sent = off_parts(pieces, part)
        sent = at("k1" + "ab"[k], sent)
        offs.append([kept + to_partner(sent)])
    for step in range(1, planes):
        for k, part in enumerate(offs):
            part.append(at(f"y{step}" + "ab"[k], onward(part[-1])))
    while len(strips) < planes:
        strips.append(Strip(joined_panel(len(strips))))
    turned = [strip.finish() for strip in strips]
    diag = []
    for (start, _), part in zip(cuts, offs):
        total = diag_first(turned[:-1], part[:-1])
        kept, sent = diag_last(member[None], total, inv_diag, start, turned[-1], part[-1])
        diag.append(kept - to_partner(sent))
    return jnp.concatenate([part[0] for part in offs], axis=1), jnp.concatenate(diag, axis=1)


def solution(mesh):
    rows, cols = mesh.shape["row"], mesh.shape["col"]
    placed = (P("row", "col"), P("row", "col"), P("row"), P("row", "col"))
    return jax.shard_map(
        functools.partial(shards, rows // MEMBERS, cols),
        mesh=mesh,
        in_specs=placed,
        out_specs=(P("row", "col"), P("row", "col")),
        check_vma=False,
    )
```
